256 devices in a mesh: dp: 8 (over x, y_hi), tm: 32 (over y_lo, z, core).
Axes of the slice: x: 4, y: 4 (y_hi: 2, y_lo: 2; y = y_hi * 2 + y_lo), z: 8, core: 2. Of those that a mesh axis runs over, the one named last changes fastest.
Arguments:
- qkv: bfloat16 [8, 3, 12544, 1536], P('dp', None, 'tm'), may hold values from -12 to 12
- w_out: bfloat16 [1536, 1536], P('dp'), may hold values from -0.15625 to 0.15625
- d_out: bfloat16 [8, 12544, 1536], P('dp', 'tm'), may hold values from -6 to 6
- clip_ids: int32 [8, 256], P('dp'), may hold values from 0 to 3, never falling along the last dimension, each value on 1 to 128 neighbouring positions
Outputs:
- mixed: bfloat16 [8, 12544, 1536], P('dp', 'tm')
- d_qkv: bfloat16 [8, 3, 12544, 1536], P('dp', None, 'tm')
- d_weight: float32 [1536, 1536], P('tm', 'dp')
The draws below stay inside these ranges and needn't reach their ends.
Inputs may be any that keep to these rules, and one draw needn't show every extreme that they name: `clip_ids`: clip numbers never fall along the frames of a sequence; a clip spans at most half of the 256 frames.
All inputs are finite; a program needn't handle non-finite values.
Results may differ from the reference program's by a relative error of at most 0.0065.
Values may be sent and summed in bfloat16 or wider, within the bound.
A program may use at most 192 MiB of HBM per device.

```python
import math
import jax
import jax.numpy as jnp
import numpy as np
from jax import lax

HEADS = 24
HEAD_DIM = 64
D = 1536
WIN_T = 8
SPATIAL = 49
SHIFT = 4
SEGMENTS = 4
FRAMES = 256
TOKENS = 12544
SEQS = 8


def draw_qkv(key, part):
    key = jax.random.fold_in(key, 11)
    subkeys = jax.random.split(key, 1)
    full_shape = (SEQS, 3, TOKENS, D)
    drawn = 1.5 * jax.random.truncated_normal(subkeys[0], -4.0, 4.0, full_shape, jnp.float32)
    return drawn.astype(jnp.bfloat16)


def levels(rng, shape, pieces, least, high):
    loudness = 1.0
    for axis_at, parts in pieces:
        heights = jax.random.uniform(jax.random.fold_in(jax.random.fold_in(rng, 6), axis_at), (parts,), jnp.float32, least / len(pieces), high / len(pieces))
        loudness = loudness * jnp.repeat(jnp.exp(heights), shape[axis_at] // parts).reshape((-1,) + (1,) * (len(shape) - 1 - axis_at))
    return loudness


def length_profile(count, total, limit, lean):
    weights = [(1 << 20) // math.isqrt(standing ** lean) + 1 for standing in range(2, count + 1)]
    rest, given = total - limit - (count - 1), [1] * (count - 1)
    while rest > 0:
        free = [i for i in range(count - 1) if given[i] < limit]
        mass, left = sum([weights[i] for i in free]), rest
        for i in free:
            addition = min(limit - given[i], max(1, left * weights[i] // mass), rest)
            given[i] = given[i] + addition
            rest = rest - addition
    return np.array([limit] + given)


def uneven_parts(key, count, total, most, skew):
    if count == 2:
        one = jax.random.randint(key, (), max(1, total - most), min(most, total - 1) + 1)
        return jnp.stack([one, total - one])
    lengths = jnp.asarray(length_profile(count, total, most, skew), jnp.int32)
    twos = (count - 1) // 2
    donor, receiver = lengths[1:1 + 2 * twos:2], lengths[2:2 + 2 * twos:2]
    slack = jnp.minimum(donor - 1, most - receiver)
    passed = jax.random.randint(jax.random.fold_in(key, 1), (twos,), 0, 1 << 20) % (slack + 1)
    lengths = lengths.at[1:1 + 2 * twos:2].set(donor - passed).at[2:2 + 2 * twos:2].set(receiver + passed)
    return lengths[jax.random.permutation(jax.random.fold_in(key, 2), count)]


def bell_draw(rng, shape, width, bound, cuts=(), held_as=jnp.bfloat16):
    entries = width * jax.random.normal(rng, shape, jnp.float32)
    if cuts:
        entries = entries * levels(rng, shape, cuts, -0.22, 0.18)
    return jnp.clip(entries, -bound, bound).astype(held_as)


def setup_inputs(seed: int = 0) -> dict:
    splits = jax.random.split(jax.random.key(seed), 5)
    qkv = draw_qkv(jax.random.fold_in(splits[4], 71), 0)
    w_out = bell_draw(splits[1], (D, D), D ** -0.5, 0.15625, ((0, 8),))
    d_out = bell_draw(splits[2], (SEQS, TOKENS, D), 1.0, 6.0, ((0, 8), (1, 32)))
    clip_ids = jax.vmap(lambda own: jnp.searchsorted(jnp.cumsum(uneven_parts(own, SEGMENTS, FRAMES, FRAMES // 2, 0)), jnp.arange(FRAMES), side="right"))(jax.random.split(splits[3], SEQS)).reshape((SEQS, FRAMES)).astype(jnp.int32)
    return {"qkv": qkv, "w_out": w_out, "d_out": d_out, "clip_ids": clip_ids}


NEG_FILL = -1e+30

def settle(values):
    return lax.optimization_barrier(values.astype(jnp.bfloat16)).astype(jnp.float32)

def window_pass(queries, keys_in, values, attn_cot, allowed):
    score_scale = HEAD_DIM ** (-0.5)
    queries_f = queries.astype(jnp.float32)
    keys_f = keys_in.astype(jnp.float32)
    values_f = values.astype(jnp.float32)
    cot_f = attn_cot.astype(jnp.float32)
    scores = jnp.einsum('wqge,wkge->wgqk', queries_f, keys_f) * score_scale
    scores = jnp.where(allowed[:, None], scores, NEG_FILL)
    row_max = lax.optimization_barrier(jnp.max(scores, axis=-1, keepdims=True))
    exp_scores = jnp.exp(scores - row_max)
    attn_probs = exp_scores / lax.optimization_barrier(jnp.sum(exp_scores, axis=-1, keepdims=True))
    probs_low = settle(attn_probs)
    attended = jnp.einsum('wgqk,wkge->wqge', probs_low, values_f).astype(jnp.bfloat16)
    grad_probs = jnp.einsum('wqge,wkge->wgqk', cot_f, values_f)
    row_total = lax.optimization_barrier(jnp.sum(attn_probs * grad_probs, axis=-1, keepdims=True))
    grad_scores = settle(attn_probs * (grad_probs - row_total))
    grad_query = (jnp.einsum('wgqk,wkge->wqge', grad_scores, keys_f) * score_scale).astype(jnp.bfloat16)
    grad_keys = (jnp.einsum('wgqk,wqge->wkge', grad_scores, queries_f) * score_scale).astype(jnp.bfloat16)
    grad_values = jnp.einsum('wgqk,wqge->wkge', probs_low, cot_f).astype(jnp.bfloat16)
    return (attended, grad_query, grad_keys, grad_values)

def split_groups(tokens_d, win_count):
    shaped = tokens_d.reshape(win_count, WIN_T * SPATIAL, HEADS // 2, 2, HEAD_DIM)
    return shaped.transpose(2, 0, 1, 3, 4)

def join_groups(grouped):
    return grouped.transpose(1, 2, 0, 3, 4).reshape(grouped.shape[1] * grouped.shape[2], -1)

def run_windows(rolled, rolled_cot, frame_ids):
    win_count = rolled.shape[1] // (WIN_T * SPATIAL)
    token_ids = jnp.repeat(frame_ids, SPATIAL).reshape(win_count, WIN_T * SPATIAL)
    allowed = token_ids[:, :, None] == token_ids[:, None, :]

    def per_group(operands):
        return window_pass(operands[0], operands[1], operands[2], operands[3], allowed)
    results = lax.map(per_group, (split_groups(rolled[0], win_count), split_groups(rolled[1], win_count), split_groups(rolled[2], win_count), split_groups(rolled_cot, win_count)))
    attended = join_groups(results[0])
    grads = jnp.stack([join_groups(results[1]), join_groups(results[2]), join_groups(results[3])])
    return (attended, grads)

def reference(qkv, w_out, d_out, clip_ids):
    edge_tok = SHIFT * SPATIAL

    def one_sequence(operands):
        qkv_seq, ids_seq, cot_in = operands
        attn_cot = jnp.dot(cot_in, w_out.T, preferred_element_type=jnp.float32).astype(jnp.bfloat16)
        rolled = jnp.roll(qkv_seq, -edge_tok, axis=1)
        rolled_cot = jnp.roll(attn_cot, -edge_tok, axis=0)
        frame_ids = jnp.roll(ids_seq, -SHIFT)
        attended, grads = run_windows(rolled, rolled_cot, frame_ids)
        attended = jnp.roll(attended, edge_tok, axis=0)
        grads = jnp.roll(grads, edge_tok, axis=1)
        mixed = jnp.dot(attended, w_out, preferred_element_type=jnp.float32).astype(jnp.bfloat16)
        grad_term = jnp.dot(attended.T, cot_in, preferred_element_type=jnp.float32)
        return (mixed, grads, grad_term)
    mixed, grads, grad_terms = lax.map(one_sequence, (qkv, clip_ids, d_out))
    norm_factor = 1.0 / math.sqrt(SEQS * TOKENS)
    d_weight = lax.optimization_barrier(jnp.sum(grad_terms, axis=0)) * norm_factor
    return (mixed, grads, d_weight)
```

```python
import functools
import math

import jax
import jax.numpy as jnp
from jax import lax
from jax.experimental import pallas as pl
from jax.experimental.pallas import tpu as pltpu
from jax.sharding import PartitionSpec as P

MESH = pl.DeviceIdType.MESH
f32, bf16 = jnp.float32, jnp.bfloat16

HEADS = 24
HEAD_DIM = 64
D = 1536
SPATIAL = 49
WIN_T = 8
FRAMES = 256
TOK = 392
HALF = 196
BLK = 208
LO = 192
QP = 256
PAIRS = HEADS // 2
CHUNK = 512
GROUP = 384
NEG = -1e30
NT = (((1,), (1,)), ((), ()))


def dot(a, b):
    return jnp.dot(a, b, preferred_element_type=f32)


def dot_nt(a, b):
    return lax.dot_general(a, b, NT, preferred_element_type=f32)


def frame_of(row):
    frame = jnp.zeros_like(row)
    for i in range(1, WIN_T):
        frame = frame + jnp.where(row >= SPATIAL * i, 1, 0)
    return frame


def cols(p, width):
    return pl.ds(pl.multiple_of(p * width, 128), width)


def kernel(
    qkv_hbm, w_hbm, dout_hbm, clip_ref,
    mixed_hbm, dqkv_hbm, dw_ref,
    qkv_s, dout_s, kv_win, q_win, dwin, w_all, probs, o_f32, o_rows, att_win,
    cot_win, ds_s, dkv_win, rdkv, dq_win, kaug, qaug,
    g_all, acc, sa1, sb1, sc1, ra1, rb1, rc1, sa2, sb2, sc2, ra2, rb2, rc2,
    fin, zs, zr, fs, fr,
    loc, hs, hr, wxs, wxr, wbs, wbr, ds_sem, dr_sem, os_sem, or_sem,
    gs, gr, r1s, r1r, r2s, r2r, zss, zrs, fss, frs,
):
    dp, tm = lax.axis_index("dp"), lax.axis_index("tm")
    x, yh = dp // 2, dp % 2
    yl, z, core = tm // 16, (tm // 2) % 8, tm % 2
    y = yh * 2 + yl
    step = 1 - 2 * core

    def at(x_, y_, z_, c_):
        return (x_ * 2 + y_ // 2, (y_ % 2) * 16 + z_ * 2 + c_)

    def along_x(d):
        return at((x + d + 4) % 4, y, z, core)

    def along_y(d):
        return at(x, (y + d + 4) % 4, z, core)

    prev, nxt = (dp, (tm + 31) % 32), (dp, (tm + 1) % 32)
    sib = (dp, tm + step)
    y_mate = at(x, 3 - y, z, core)
    final_mate = (dp + 1 - 2 * yh, tm)

    def rcopy(src, dst, ssem, rsem, dev):
        return pltpu.make_async_remote_copy(
            src_ref=src, dst_ref=dst, send_sem=ssem, recv_sem=rsem, device_id=dev, device_id_type=MESH
        )

    loads = [
        pltpu.make_async_copy(qkv_hbm.at[1], qkv_s.at[1], loc.at[1]),
        pltpu.make_async_copy(qkv_hbm.at[2], qkv_s.at[2], loc.at[2]),
        pltpu.make_async_copy(qkv_hbm.at[0], qkv_s.at[0], loc.at[0]),
        pltpu.make_async_copy(dout_hbm, dout_s, loc.at[3]),
        pltpu.make_async_copy(w_hbm, w_all.at[pl.ds(pl.multiple_of(dp * 192, 192), 192)], loc.at[4]),
    ]
    for load in loads:
        load.start()

    barrier = pltpu.get_barrier_semaphore()
    peers = [prev, nxt, along_x(1), along_x(2), along_x(3), along_y(1), along_y(3), final_mate]
    peers += [at(x, y, (z + d) % 8, core) for d in range(1, 8)]
    for dev in peers:
        pl.semaphore_signal(barrier, inc=1, device_id=dev, device_id_type=MESH)
    pl.semaphore_wait(barrier, len(peers))

    def w_rows(src_dp, half):
        return pl.ds(pl.multiple_of(src_dp * 192 + half * 96, 96), 96)

    other = dp + 1 - 2 * yh
    mine = w_hbm.at[pl.ds(pl.multiple_of(core * 96, 96), 96)]

    def w_y():
        return rcopy(mine, w_all.at[w_rows(dp, core)], wxs.at[0], wxr.at[0], y_mate)

    def w_x(d, which):
        i = d if which == 0 else 3 + d
        if which == 0:
            return rcopy(mine, w_all.at[w_rows(dp, core)], wxs.at[i], wxr.at[i], along_x(d))
        rows = w_rows(other, core)
        return rcopy(w_all.at[rows], w_all.at[rows], wxs.at[i], wxr.at[i], along_x(d))

    def w_sib(d, which):
        i = d if which == 0 else 3 + d
        src = ((x + 4 - d) % 4) * 2 + (yh if which == 0 else 1 - yh)
        rows = w_rows(src, core)
        return rcopy(w_all.at[rows], w_all.at[rows], wbs.at[i], wbr.at[i], sib)

    def w_sib_y():
        rows = w_rows(other, core)
        return rcopy(w_all.at[rows], w_all.at[rows], wbs.at[0], wbr.at[0], sib)

    w_y().start()

    loads[0].wait()
    loads[1].wait()
    for t in range(2):
        kv_win[0, t, BLK:, :] = qkv_s[1 + t, 0:BLK, :]
        kv_win[1, t, 0:192, :] = qkv_s[1 + t, LO:384, :]
        kv_win[1, t, 192:200, :] = qkv_s[1 + t, 384:392, :]
        kv_win[1, t, 200:208, :] = jnp.zeros((8, D), bf16)

    def halo(to_next, c):
        if to_next:
            part = kv_win.at[1, :, 0:BLK, c * CHUNK : (c + 1) * CHUNK]
            there = kv_win.at[0, :, 0:BLK, c * CHUNK : (c + 1) * CHUNK]
            return rcopy(part, there, hs.at[0, c], hr.at[0, c], nxt)
        part = kv_win.at[0, :, BLK : 2 * BLK, c * CHUNK : (c + 1) * CHUNK]
        there = kv_win.at[1, :, BLK : 2 * BLK, c * CHUNK : (c + 1) * CHUNK]
        return rcopy(part, there, hs.at[1, c], hr.at[1, c], prev)

    for c in range(3):
        halo(True, c).start()
        halo(False, c).start()
    for d in (1, 3, 2):
        w_x(d, 0).start()

    loads[2].wait()
    q_win[0, 0:BLK, :] = qkv_s[0, 0:BLK, :] * jnp.asarray(0.125, bf16)
    q_win[1, 0:192, :] = qkv_s[0, LO:384, :] * jnp.asarray(0.125, bf16)
    q_win[1, 192:200, :] = qkv_s[0, 384:392, :] * jnp.asarray(0.125, bf16)
    q_win[1, 200:208, :] = jnp.zeros((8, D), bf16)
    q_win[:, BLK:, :] = jnp.zeros((2, QP - BLK, D), bf16)

    loads[3].wait()
    row16 = lax.broadcasted_iota(jnp.int32, (16, D), 0)
    zero16 = jnp.zeros((16, D), f32)
    edge = dout_s[192:208, :].astype(f32)
    dwin[0, 0:192, :] = dout_s[0:192, :]
    dwin[0, 192:208, :] = jnp.where(row16 < HALF - LO, edge, zero16).astype(bf16)
    dwin[0, 208:256, :] = jnp.zeros((48, D), bf16)
    dwin[0, 256:272, :] = jnp.where(row16 >= HALF - LO, edge, zero16).astype(bf16)
    dwin[0, 272:448, :] = dout_s[208:384, :]
    dwin[0, 448:456, :] = dout_s[384:392, :]
    dwin[0, 456:464, :] = jnp.zeros((8, D), bf16)
    dwin[0, 464:512, :] = jnp.zeros((48, D), bf16)
    cot_win[:, BLK:, :] = jnp.zeros((2, QP - BLK, GROUP), bf16)

    def d_copy():
        return rcopy(dwin.at[0], dwin.at[1], ds_sem.at[0], dr_sem.at[0], sib)

    d_copy().start()

    row = lax.broadcasted_iota(jnp.int32, (BLK, 128), 0)
    lane = lax.broadcasted_iota(jnp.int32, (BLK, 128), 1)
    row_q = lax.broadcasted_iota(jnp.int32, (QP, 128), 0)
    lane_q = lax.broadcasted_iota(jnp.int32, (QP, 128), 1)
    for half in range(2):
        clips = [clip_ref[0, (tm * 8 + FRAMES - 4 + 8 * half + w) % FRAMES] for w in range(WIN_T)]
        of_lane = jnp.full((BLK, 128), -1, jnp.int32)
        for w in range(WIN_T):
            of_lane = jnp.where(lane == w, clips[w], of_lane)
        for part in range(2):
            if part == 0:
                frame, real = frame_of(row + LO) - 4, jnp.logical_and(row >= HALF - LO, row < TOK - LO)
            else:
                frame, real = frame_of(row) + 4, row < HALF
            of_row = jnp.full((BLK, 128), -2, jnp.int32)
            for w in range(WIN_T):
                of_row = jnp.where(frame == w, clips[w], of_row)
            seen = jnp.logical_and(real, of_row == of_lane)
            bias = jnp.where(jnp.logical_or(seen, lane >= WIN_T), 0.0, NEG)
            kaug[half, part * BLK : (part + 1) * BLK, :] = bias.astype(bf16)
        if half == 0:
            frame, real = frame_of(row_q) + 4, row_q < HALF
        else:
            frame = frame_of(row_q + LO) - 4
            real = jnp.logical_and(row_q >= HALF - LO, row_q < TOK - LO)
        qaug[half] = jnp.where(jnp.logical_and(real, lane_q == frame), 1.0, 0.0).astype(bf16)

    low = lane_q < HEAD_DIM
    none = jnp.zeros((QP, 128), bf16)
    q_lane = lax.broadcasted_iota(jnp.int32, (1, QP), 1)

    def pick(value, h):
        return jnp.where(low, value, none) if h == 0 else jnp.where(low, none, value)

    def forward(half, p):
        c = cols(p, 128)
        q = q_win[half, :, c]
        keys = jnp.concatenate([kv_win[half, 0, :, c], kaug[half]], axis=1)
        marks = qaug[half]
        for h in range(2):
            s = dot_nt(keys, jnp.concatenate([pick(q, h), marks], axis=1))
            e = jnp.exp(s - jnp.max(s, axis=0, keepdims=True))
            total = jnp.sum(e, axis=0, keepdims=True)
            probs[half, p, h] = (e * (1.0 / total)).astype(bf16)
        start = jnp.where(half == 0, 0, HALF - LO)
        valid = jnp.logical_and(q_lane >= start, q_lane < start + HALF).astype(f32)
        vt = kv_win[half, 1, :, c].T
        outs = []
        for h in range(2):
            outs.append(dot(vt[64 * h : 64 * h + 64], probs[half, p, h]) * valid)
        o = jnp.concatenate(outs, axis=0)
        o_f32[half, pl.ds(pl.multiple_of(p * 128, 128), 128), :] = o
        low_o = o.astype(bf16)
        for j in range(8):
            r = p * 8 + j
            o_rows[r // 6, r % 6, :, cols(half, QP)] = low_o[16 * j : 16 * j + 16]
        att_win[half, :, c] = low_o.T[0:BLK]

    def o_copy(half):
        rows = pl.ds(3 * (1 - core), 3)
        return rcopy(
            o_rows.at[:, rows, :, cols(half, QP)],
            o_rows.at[:, rows, :, pl.ds(pl.multiple_of(512 + half * QP, QP), QP)],
            os_sem.at[half], or_sem.at[half], sib,
        )

    for turn in range(2):
        half = 1 - core if turn == 0 else core
        for c in range(3):
            pltpu.make_async_remote_copy(
                src_ref=kv_win.at[0, :, 0:BLK, 0:CHUNK],
                dst_ref=kv_win.at[half, :, pl.ds(pl.multiple_of(half * BLK, BLK), BLK), c * CHUNK : (c + 1) * CHUNK],
                send_sem=hs.at[0, c], recv_sem=hr.at[half, c], device_id=nxt, device_id_type=MESH,
            ).wait_recv()

            @pl.loop(0, 4)
            def _(i):
                forward(half, c * 4 + i)

        o_copy(half).start()
        if turn == 0:
            w_y().wait_recv()
            w_sib_y().start()
            for d in (1, 3, 2):
                w_x(d, 1).start()

    d_copy().wait_recv()
    o_copy(0).wait_recv()
    o_copy(1).wait_recv()

    @pl.loop(0, 4)
    def _(i):
        lhs = o_rows[:, pl.ds(3 * core, 3), :, :].reshape(768, 1024)
        rhs = dwin[:, :, cols(i, GROUP)].reshape(1024, GROUP)
        g_all[i] = dot(lhs, rhs)

    def ring_dev(axis, d):
        return along_y(d) if axis == 0 else along_x(d)

    def ring_at(axis, d):
        if axis == 0:
            to = (y + 4 + d * step) % 4
            return (to % 2) * 2 + to // 2
        return (x + 4 + d * step) % 4

    def piece1(inst, d):
        where = ring_at(inst, d)
        if inst == 0:
            return g_all[:, pl.ds(pl.multiple_of(where * 192, 96), 96), :]
        return jnp.stack([g_all[where, r * 192 + 96 : r * 192 + 192, :] for r in range(4)])

    def send1(inst, kind):
        src, dst = ((sa1, ra1), (sb1, rb1), (sc1, rc1))[kind]
        dev = ring_dev(inst, step if kind < 2 else -step)
        return rcopy(src.at[inst], dst.at[inst], r1s.at[inst, kind], r1r.at[inst, kind], dev)

    def send2(inst, kind):
        src, dst = ((sa2, ra2), (sb2, rb2), (sc2, rc2))[kind]
        dev = ring_dev(1 - inst, step if kind < 2 else -step)
        return rcopy(src.at[inst], dst.at[inst], r2s.at[inst, kind], r2r.at[inst, kind], dev)

    def sum1_start():
        for inst in range(2):
            sa1[inst] = piece1(inst, 2).astype(bf16)
            send1(inst, 0).start()
            sc1[inst] = piece1(inst, -1).astype(bf16)
            send1(inst, 2).start()

    def sum1_mid():
        for inst in range(2):
            send1(inst, 0).wait_recv()
            sb1[inst] = (piece1(inst, 1) + ra1[inst].astype(f32)).astype(bf16)
            send1(inst, 1).start()

    def sum2_start():
        for inst in range(2):
            send1(inst, 1).wait_recv()
            send1(inst, 2).wait_recv()
            acc[inst] = piece1(inst, 0) + rb1[inst].astype(f32) + rc1[inst].astype(f32)
            sa2[inst] = acc[inst, ring_at(1 - inst, 2)].astype(bf16)
            send2(inst, 0).start()
            sc2[inst] = acc[inst, ring_at(1 - inst, -1)].astype(bf16)
            send2(inst, 2).start()

    def sum2_mid():
        for inst in range(2):
            send2(inst, 0).wait_recv()
            sb2[inst] = (acc[inst, ring_at(1 - inst, 1)] + ra2[inst].astype(f32)).astype(bf16)
            send2(inst, 1).start()

    def z_copy(j):
        to = yh * 4 + j
        slot = (to + 8 - z) % 8
        return to, rcopy(zs.at[j], zr.at[slot], zss.at[j], zrs.at[slot], at(x, y, to, core))

    def sum3_start():
        for inst in range(2):
            send2(inst, 1).wait_recv()
            send2(inst, 2).wait_recv()
            done = acc[inst, ring_at(1 - inst, 0)] + rb2[inst].astype(f32) + rc2[inst].astype(f32)
            for jj in range(2):
                j = inst * 2 + jj
                fin[j] = done[jj * 48 : jj * 48 + 48]
                zs[j] = done[jj * 48 : jj * 48 + 48].astype(bf16)
                to, copy = z_copy(j)
                pl.when(to != z)(copy.start)

    norm = 1.0 / math.sqrt(8 * 32 * TOK)
    keeper = z // 4 == yh

    def f_copy():
        return rcopy(fs, fr, fss.at[0], frs.at[0], final_mate)

    def sum_end():
        @pl.when(keeper)
        def _():
            total = fin[z % 4]
            for d in range(1, 8):
                rcopy(zs.at[0], zr.at[d], zss.at[0], zrs.at[d], sib).wait_recv()
                total = total + zr[d].astype(f32)
            total = total * norm
            left, right = total[:, 0:192], total[:, 192:384]
            dw_ref[...] = jnp.where(yh == 0, left, right)
            fs[...] = jnp.where(yh == 0, right, left)
            f_copy().start()

    def sum_last():
        @pl.when(jnp.logical_not(keeper))
        def _():
            f_copy().wait_recv()
            dw_ref[...] = fr[...]

    sum1_start()

    loads[4].wait()
    order = (0, 1, 3, 2)

    def backward(half, p, i):
        c = cols(p, 128)
        do = cot_win[half, :, cols(i, 128)]
        keys, values = kv_win[half, 0, :, c], kv_win[half, 1, :, c]
        q = q_win[half, :, c]
        prod = do.T.astype(f32) * o_f32[half, pl.ds(pl.multiple_of(p * 128, 128), 128), :]
        for h in range(2):
            grad = dot_nt(values, pick(do, h))
            total = jnp.sum(prod[64 * h : 64 * h + 64], axis=0, keepdims=True)
            ds_s[half, h] = (probs[half, p, h].astype(f32) * (grad - total)).astype(bf16)
        kt = keys.T
        dq = jnp.concatenate([dot(kt[64 * h : 64 * h + 64], ds_s[half, h]) for h in range(2)], axis=0) * 0.125
        dq_win[half, :, c] = dq.astype(bf16).T[0:BLK]
        dkv_win[half, 1, :, c] = (dot(probs[half, p, 0], pick(do, 0)) + dot(probs[half, p, 1], pick(do, 1))).astype(bf16)
        dkv_win[half, 0, :, c] = (dot(ds_s[half, 0], pick(q, 0)) + dot(ds_s[half, 1], pick(q, 1))).astype(bf16)

    def g_copy(to_next, k):
        c = cols((x + 4 - order[k]) % 4, GROUP)
        if to_next:
            return rcopy(dkv_win.at[1, :, BLK : 2 * BLK, c], rdkv.at[0, :, :, c], gs.at[0, k], gr.at[0, k], nxt)
        return rcopy(dkv_win.at[0, :, 0:BLK, c], rdkv.at[1, :, :, c], gs.at[1, k], gr.at[1, k], prev)

    def pass_on(d):
        for which in range(2):
            w_x(d, which).wait_recv()
            w_sib(d, which).start()

    w_sib_y().wait_recv()
    for k, d in enumerate(order):
        g = (x + 4 - d) % 4
        if d:
            for which in range(2):
                w_sib(d, which).wait_recv()
        for half in range(2):
            cot_win[half, 0:BLK, :] = dot_nt(
                dwin[0, half * QP : half * QP + BLK, :], w_all[pl.ds(pl.multiple_of(g * GROUP, GROUP), GROUP), :]
            ).astype(bf16)
        if k + 1 < 4:
            pass_on(order[k + 1])

        @pl.loop(0, 3)
        def _(i):
            for half in range(2):
                backward(half, g * 3 + i, i)

        g_copy(True, k).start()
        g_copy(False, k).start()
        (sum1_mid, sum2_start, sum2_mid, sum3_start)[k]()

    @pl.loop(0, 3)
    def _(i):
        c = cols(i, 512)
        w = w_all[:, c]
        first = dot(att_win[0], w)
        second = dot(att_win[1], w)
        dout_s[0:192, c] = first[0:192].astype(bf16)
        dout_s[192:208, c] = (first[192:208] + second[0:16]).astype(bf16)
        dout_s[208:392, c] = second[16:200].astype(bf16)

    out_mixed = pltpu.make_async_copy(dout_s, mixed_hbm, loc.at[5])
    out_mixed.start()
    qkv_s[0, 0:192, :] = dq_win[0, 0:192, :]
    qkv_s[0, 192:208, :] = dq_win[0, 192:208, :] + dq_win[1, 0:16, :]
    qkv_s[0, 208:392, :] = dq_win[1, 16:200, :]
    out_q = pltpu.make_async_copy(qkv_s.at[0], dqkv_hbm.at[0], loc.at[6])
    out_q.start()
    sum_end()
    for k in range(4):
        g_copy(True, k).wait_recv()
        g_copy(False, k).wait_recv()
    outs = []
    for t in range(2):
        first = dkv_win[0, t, BLK:, :].astype(f32) + rdkv[0, t].astype(f32)
        second = dkv_win[1, t, 0:BLK, :].astype(f32) + rdkv[1, t].astype(f32)
        qkv_s[1 + t, 0:192, :] = first[0:192].astype(bf16)
        qkv_s[1 + t, 192:208, :] = (first[192:208] + second[0:16]).astype(bf16)
        qkv_s[1 + t, 208:392, :] = second[16:200].astype(bf16)
        outs.append(pltpu.make_async_copy(qkv_s.at[1 + t], dqkv_hbm.at[1 + t], loc.at[7 + t]))
        outs[t].start()
    sum_last()

    w_y().wait_send()
    w_sib_y().wait_send()
    for d in (1, 2, 3):
        for which in range(2):
            w_x(d, which).wait_send()
            w_sib(d, which).wait_send()
    for c in range(3):
        halo(True, c).wait_send()
        halo(False, c).wait_send()
    d_copy().wait_send()
    for half in range(2):
        o_copy(half).wait_send()
    for k in range(4):
        g_copy(True, k).wait_send()
        g_copy(False, k).wait_send()
    for inst in range(2):
        for kind in range(3):
            send1(inst, kind).wait_send()
            send2(inst, kind).wait_send()
    for j in range(4):
        to, copy = z_copy(j)
        pl.when(to != z)(copy.wait_send)
    pl.when(keeper)(lambda: f_copy().wait_send())
    out_mixed.wait()
    out_q.wait()
    for out in outs:
        out.wait()


def per_device(qkv, w_out, d_out, clip_ids):
    hbm = pl.BlockSpec(memory_space=pl.ANY)
    vmem = pltpu.VMEM
    dma = pltpu.SemaphoreType.DMA
    mixed, grads, d_weight = pl.pallas_call(
        kernel,
        in_specs=[hbm, hbm, hbm, pl.BlockSpec(memory_space=pltpu.SMEM)],
        out_specs=[hbm, hbm, pl.BlockSpec(memory_space=pltpu.VMEM)],
        out_shape=[
            jax.ShapeDtypeStruct((TOK, D), bf16),
            jax.ShapeDtypeStruct((3, TOK, D), bf16),
            jax.ShapeDtypeStruct((48, 192), f32),
        ],
        scratch_shapes=[
            vmem((3, TOK, D), bf16),
            vmem((TOK, D), bf16),
            vmem((2, 2, 2 * BLK, D), bf16),
            vmem((2, QP, D), bf16),
            vmem((2, 2 * QP, D), bf16),
            vmem((D, D), bf16),
            vmem((2, PAIRS, 2, 2 * BLK, QP), bf16),
            vmem((2, D, QP), f32),
            vmem((16, 6, 16, 4 * QP), bf16),
            vmem((2, BLK, D), bf16),
            vmem((2, QP, GROUP), bf16),
            vmem((2, 2, 2 * BLK, QP), bf16),
            vmem((2, 2, 2 * BLK, D), bf16),
            vmem((2, 2, BLK, D), bf16),
            vmem((2, BLK, D), bf16),
            vmem((2, 2 * BLK, 128), bf16),
            vmem((2, QP, 128), bf16),
            vmem((4, 768, GROUP), f32),
            vmem((2, 4, 96, GROUP), f32),
        ]
        + [vmem((2, 4, 96, GROUP), bf16)] * 6
        + [vmem((2, 96, GROUP), bf16)] * 6
        + [
            vmem((4, 48, GROUP), f32),
            vmem((4, 48, GROUP), bf16),
            vmem((8, 48, GROUP), bf16),
            vmem((48, 192), f32),
            vmem((48, 192), f32),
            dma((9,)),
            dma((2, 3)), dma((2, 3)),
            dma((7,)), dma((7,)), dma((7,)), dma((7,)),
            dma((1,)), dma((1,)), dma((2,)), dma((2,)),
            dma((2, 4)), dma((2, 4)),
            dma((2, 3)), dma((2, 3)), dma((2, 3)), dma((2, 3)),
            dma((4,)), dma((8,)), dma((1,)), dma((1,)),
        ],
        compiler_params=pltpu.CompilerParams(
            collective_id=0, has_side_effects=True, vmem_limit_bytes=62 << 20
        ),
    )(qkv[0], w_out, d_out[0], clip_ids)
    return mixed[None], grads[None], d_weight


def solution(mesh):
    return jax.shard_map(
        per_device,
        mesh=mesh,
        in_specs=(P("dp", None, "tm", None), P("dp", None), P("dp", "tm", None), P("dp", None)),
        out_specs=(P("dp", "tm", None), P("dp", None, "tm", None), P("tm", "dp")),
        check_vma=False,
    )
```

```python
import functools
import math

import jax
import jax.numpy as jnp
from jax import lax
from jax.experimental import pallas as pl
from jax.experimental.pallas import tpu as pltpu
from jax.sharding import PartitionSpec as P

MESH = pl.DeviceIdType.MESH
f32, bf16 = jnp.float32, jnp.bfloat16

HEADS = 24
HEAD_DIM = 64
D = 1536
SPATIAL = 49
WIN_T = 8
FRAMES = 256
TOK = 392
HALF = 196
BLK = 208
LO = 192
QP = 256
PAIRS = HEADS // 2
CHUNK = 256
STEPS = D // CHUNK
PER = CHUNK // 128
GROUP = 384
NEG = -1e30
NT = (((1,), (1,)), ((), ()))


def dot(a, b):
    return jnp.dot(a, b, preferred_element_type=f32)


def dot_nt(a, b):
    return lax.dot_general(a, b, NT, preferred_element_type=f32)


def frame_of(row):
    frame = jnp.zeros_like(row)
    for i in range(1, WIN_T):
        frame = frame + jnp.where(row >= SPATIAL * i, 1, 0)
    return frame


def cols(p, width):
    return pl.ds(pl.multiple_of(p * width, 128), width)


def kernel(
    qkv_hbm, w_hbm, dout_hbm, clip_ref,
    mixed_hbm, dqkv_hbm, dw_ref,
    qkv_s, dout_s, kv_win, q_win, dwin, w_all, probs, o_f32, o_rows, att_win,
    cot_win, ds_s, dkv_win, rdkv, dq_win, kaug, qaug,
    g_all, acc, sa1, sb1, sc1, ra1, rb1, rc1, sa2, sb2, sc2, ra2, rb2, rc2,
    fin, zs, zr, fs, fr,
    loc, hs, hr, ws, wr, wbs, wbr, ds_sem, dr_sem, os_sem, or_sem,
    gs, gr, r1s, r1r, r2s, r2r, zss, zrs, fss, frs,
):
    dp, tm = lax.axis_index("dp"), lax.axis_index("tm")
    x, yh = dp // 2, dp % 2
    yl, z, core = tm // 16, (tm // 2) % 8, tm % 2
    y = yh * 2 + yl
    step = 1 - 2 * core

    def at(x_, y_, z_, c_):
        return (x_ * 2 + y_ // 2, (y_ % 2) * 16 + z_ * 2 + c_)

    def along_x(d):
        return at((x + d + 4) % 4, y, z, core)

    def along_y(d):
        return at(x, (y + d + 4) % 4, z, core)

    prev, nxt = (dp, (tm + 31) % 32), (dp, (tm + 1) % 32)
    sib = (dp, tm + step)
    final_mate = (dp + 1 - 2 * yh, tm)

    across = at(x, 3 - y, z, core)

    def rcopy(src, dst, ssem, rsem, dev):
        return pltpu.make_async_remote_copy(
            src_ref=src, dst_ref=dst, send_sem=ssem, recv_sem=rsem, device_id=dev, device_id_type=MESH
        )

    loads = [
        pltpu.make_async_copy(qkv_hbm.at[1], qkv_s.at[1], loc.at[1]),
        pltpu.make_async_copy(qkv_hbm.at[2], qkv_s.at[2], loc.at[2]),
        pltpu.make_async_copy(qkv_hbm.at[0], qkv_s.at[0], loc.at[0]),
        pltpu.make_async_copy(dout_hbm, dout_s, loc.at[3]),
        pltpu.make_async_copy(
            w_hbm, w_all.at[pl.ds(pl.multiple_of(dp * 192, 192), 192)], loc.at[4]
        ),
    ]
    for load in loads:
        load.start()

    barrier = pltpu.get_barrier_semaphore()
    peers = [prev, nxt, along_x(1), along_x(2), along_x(3), along_y(1), along_y(2), along_y(3)]
    peers += [at(x, y, (z + d) % 8, core) for d in range(1, 8)]
    for dev in peers:
        pl.semaphore_signal(barrier, inc=1, device_id=dev, device_id_type=MESH)

    def w_rows(d, which):
        src = ((x + 4 - d) % 4) * 2 + (yh if which == 0 else 1 - yh)
        return w_all.at[pl.ds(pl.multiple_of(src * 192 + core * 96, 96), 96)]

    def w_copy(d, which):
        if (d, which) == (0, 1):
            rows, dev = w_rows(0, 0), across
        elif (d, which) == (2, 1):
            rows, dev = w_rows(2, 0), across
        else:
            rows, dev = w_rows(0, which), along_x(d)
        return rcopy(rows, rows, ws.at[d, which], wr.at[d, which], dev)

    def w_sib(d, which):
        rows = w_rows(d, which)
        return rcopy(rows, rows, wbs.at[d, which], wbr.at[d, which], sib)

    def w_arrived(d, which):
        w_copy(d, which).wait_recv()
        w_sib(d, which).start()

    pieces = [(0, 1)] + [(d, which) for d in (1, 3, 2) for which in range(2)]

    loads[0].wait()
    loads[1].wait()
    for t in range(2):
        kv_win[0, t, BLK:, :] = qkv_s[1 + t, 0:BLK, :]
        kv_win[1, t, 0:192, :] = qkv_s[1 + t, LO:384, :]
        kv_win[1, t, 192:200, :] = qkv_s[1 + t, 384:392, :]
        kv_win[1, t, 200:208, :] = jnp.zeros((8, D), bf16)

    def halo(to_next, c):
        if to_next:
            part = kv_win.at[1, :, 0:BLK, c * CHUNK : (c + 1) * CHUNK]
            there = kv_win.at[0, :, 0:BLK, c * CHUNK : (c + 1) * CHUNK]
            return rcopy(part, there, hs.at[0, c], hr.at[0, c], nxt)
        part = kv_win.at[0, :, BLK : 2 * BLK, c * CHUNK : (c + 1) * CHUNK]
        there = kv_win.at[1, :, BLK : 2 * BLK, c * CHUNK : (c + 1) * CHUNK]
        return rcopy(part, there, hs.at[1, c], hr.at[1, c], prev)

    pl.semaphore_wait(barrier, len(peers))
    for c in range(STEPS):
        halo(True, c).start()
        halo(False, c).start()
    loads[4].wait()
    for piece in ((0, 1), (1, 0), (3, 0), (2, 0)):
        w_copy(*piece).start()

    loads[2].wait()
    q_win[0, 0:BLK, :] = qkv_s[0, 0:BLK, :] * jnp.asarray(0.125, bf16)
    q_win[1, 0:192, :] = qkv_s[0, LO:384, :] * jnp.asarray(0.125, bf16)
    q_win[1, 192:200, :] = qkv_s[0, 384:392, :] * jnp.asarray(0.125, bf16)
    q_win[1, 200:208, :] = jnp.zeros((8, D), bf16)
    q_win[:, BLK:, :] = jnp.zeros((2, QP - BLK, D), bf16)

    loads[3].wait()
    row16 = lax.broadcasted_iota(jnp.int32, (16, D), 0)
    zero16 = jnp.zeros((16, D), f32)
    edge = dout_s[192:208, :].astype(f32)
    dwin[0, 0:192, :] = dout_s[0:192, :]
    dwin[0, 192:208, :] = jnp.where(row16 < HALF - LO, edge, zero16).astype(bf16)
    dwin[0, 208:256, :] = jnp.zeros((48, D), bf16)
    dwin[0, 256:272, :] = jnp.where(row16 >= HALF - LO, edge, zero16).astype(bf16)
    dwin[0, 272:448, :] = dout_s[208:384, :]
    dwin[0, 448:456, :] = dout_s[384:392, :]
    dwin[0, 456:464, :] = jnp.zeros((8, D), bf16)
    dwin[0, 464:512, :] = jnp.zeros((48, D), bf16)
    cot_win[:, BLK:, :] = jnp.zeros((2, QP - BLK, GROUP), bf16)

    def d_copy():
        return rcopy(dwin.at[0], dwin.at[1], ds_sem.at[0], dr_sem.at[0], sib)

    d_copy().start()

    row = lax.broadcasted_iota(jnp.int32, (BLK, 128), 0)
    lane = lax.broadcasted_iota(jnp.int32, (BLK, 128), 1)
    row_q = lax.broadcasted_iota(jnp.int32, (QP, 128), 0)
    lane_q = lax.broadcasted_iota(jnp.int32, (QP, 128), 1)
    for half in range(2):
        clips = [clip_ref[0, (tm * 8 + FRAMES - 4 + 8 * half + w) % FRAMES] for w in range(WIN_T)]
        of_lane = jnp.full((BLK, 128), -1, jnp.int32)
        for w in range(WIN_T):
            of_lane = jnp.where(lane == w, clips[w], of_lane)
        for part in range(2):
            if part == 0:
                frame, real = frame_of(row + LO) - 4, jnp.logical_and(row >= HALF - LO, row < TOK - LO)
            else:
                frame, real = frame_of(row) + 4, row < HALF
            of_row = jnp.full((BLK, 128), -2, jnp.int32)
            for w in range(WIN_T):
                of_row = jnp.where(frame == w, clips[w], of_row)
            seen = jnp.logical_and(real, of_row == of_lane)
            bias = jnp.where(jnp.logical_or(seen, lane >= WIN_T), 0.0, NEG)
            kaug[half, part * BLK : (part + 1) * BLK, :] = bias.astype(bf16)
        if half == 0:
            frame, real = frame_of(row_q) + 4, row_q < HALF
        else:
            frame = frame_of(row_q + LO) - 4
            real = jnp.logical_and(row_q >= HALF - LO, row_q < TOK - LO)
        qaug[half] = jnp.where(jnp.logical_and(real, lane_q == frame), 1.0, 0.0).astype(bf16)

    low = lane_q < HEAD_DIM
    none = jnp.zeros((QP, 128), bf16)
    q_lane = lax.broadcasted_iota(jnp.int32, (1, QP), 1)

    def pick(value, h):
        return jnp.where(low, value, none) if h == 0 else jnp.where(low, none, value)

    def softmax(half, p):
        c = cols(p, 128)
        q = q_win[half, :, c]
        keys = jnp.concatenate([kv_win[half, 0, :, c], kaug[half]], axis=1)
        marks = qaug[half]
        for h in range(2):
            s = dot_nt(keys, jnp.concatenate([pick(q, h), marks], axis=1))
            e = jnp.exp(s - jnp.max(s, axis=0, keepdims=True))
            total = jnp.sum(e, axis=0, keepdims=True)
            probs[half, p, h] = (e * (1.0 / total)).astype(bf16)

    def attend(half, p):
        c = cols(p, 128)
        start = jnp.where(half == 0, 0, HALF - LO)
        valid = jnp.logical_and(q_lane >= start, q_lane < start + HALF).astype(f32)
        vt = kv_win[half, 1, :, c].T
        outs = []
        for h in range(2):
            outs.append(dot(vt[64 * h : 64 * h + 64], probs[half, p, h]) * valid)
        o = jnp.concatenate(outs, axis=0)
        o_f32[half, pl.ds(pl.multiple_of(p * 128, 128), 128), :] = o
        low_o = o.astype(bf16)
        for j in range(8):
            r = p * 8 + j
            o_rows[r // 6, r % 6, :, cols(half, QP)] = low_o[16 * j : 16 * j + 16]
        att_win[half, :, c] = low_o.T[0:BLK]

    def o_copy(half):
        rows = pl.ds(3 * (1 - core), 3)
        return rcopy(
            o_rows.at[:, rows, :, cols(half, QP)],
            o_rows.at[:, rows, :, pl.ds(pl.multiple_of(512 + half * QP, QP), QP)],
            os_sem.at[half], or_sem.at[half], sib,
        )

    def weight_grad(turn):
        own, there = (1 - core, core) if turn == 0 else (core, 1 - core)
        o_copy(there).wait_recv()

        @pl.loop(0, 4)
        def _(i):
            sub = pl.ds(3 * core, 3)
            lhs = jnp.concatenate(
                [
                    o_rows[:, sub, :, cols(own, QP)].reshape(768, QP),
                    o_rows[:, sub, :, pl.ds(pl.multiple_of(512 + there * QP, QP), QP)].reshape(768, QP),
                ],
                axis=1,
            )
            rhs = jnp.concatenate(
                [
                    dwin[0, pl.ds(pl.multiple_of(own * QP, QP), QP), cols(i, GROUP)],
                    dwin[1, pl.ds(pl.multiple_of(there * QP, QP), QP), cols(i, GROUP)],
                ],
                axis=0,
            )
            if turn == 0:
                g_all[i] = dot(lhs, rhs)
            else:
                g_all[i] += dot(lhs, rhs)

    for turn in range(2):
        half = 1 - core if turn == 0 else core
        for c in range(STEPS):
            pltpu.make_async_remote_copy(
                src_ref=kv_win.at[0, :, 0:BLK, 0:CHUNK],
                dst_ref=kv_win.at[half, :, pl.ds(pl.multiple_of(half * BLK, BLK), BLK), c * CHUNK : (c + 1) * CHUNK],
                send_sem=hs.at[0, c], recv_sem=hr.at[half, c], device_id=nxt, device_id_type=MESH,
            ).wait_recv()

            for p in range(c * PER, (c + 1) * PER):
                if c:
                    attend(half, p - PER)
            for p in range(c * PER, (c + 1) * PER):
                softmax(half, p)
            if c == STEPS - 1:
                for p in range(c * PER, (c + 1) * PER):
                    attend(half, p)

            if turn == 0 and c == 5:
                w_arrived(0, 1)
                w_copy(1, 1).start()
                w_copy(3, 1).start()
            if turn == 1 and c == 1:
                d_copy().wait_recv()
                weight_grad(0)
        o_copy(half).start()

    def ring_dev(axis, d):
        return along_y(d) if axis == 0 else along_x(d)

    def ring_at(axis, d):
        if axis == 0:
            to = (y + 4 + d * step) % 4
            return (to % 2) * 2 + to // 2
        return (x + 4 + d * step) % 4

    def piece1(inst, d):
        where = ring_at(inst, d)
        if inst == 0:
            return g_all[:, pl.ds(pl.multiple_of(where * 192, 96), 96), :]
        return jnp.stack([g_all[where, r * 192 + 96 : r * 192 + 192, :] for r in range(4)])

    def send1(inst, kind):
        src, dst = ((sa1, ra1), (sb1, rb1), (sc1, rc1))[kind]
        dev = ring_dev(inst, step if kind < 2 else -step)
        return rcopy(src.at[inst], dst.at[inst], r1s.at[inst, kind], r1r.at[inst, kind], dev)

    def send2(inst, kind):
        src, dst = ((sa2, ra2), (sb2, rb2), (sc2, rc2))[kind]
        dev = ring_dev(1 - inst, step if kind < 2 else -step)
        return rcopy(src.at[inst], dst.at[inst], r2s.at[inst, kind], r2r.at[inst, kind], dev)

    def sum1_start():
        for inst in range(2):
            sa1[inst] = piece1(inst, 2).astype(bf16)
            send1(inst, 0).start()

    def sum1_more():
        for inst in range(2):
            sc1[inst] = piece1(inst, -1).astype(bf16)
            send1(inst, 2).start()

    def sum1_mid():
        for inst in range(2):
            send1(inst, 0).wait_recv()
            sb1[inst] = (piece1(inst, 1) + ra1[inst].astype(f32)).astype(bf16)
            send1(inst, 1).start()

    def sum2_start():
        for inst in range(2):
            send1(inst, 1).wait_recv()
            send1(inst, 2).wait_recv()
            acc[inst] = piece1(inst, 0) + rb1[inst].astype(f32) + rc1[inst].astype(f32)
            sa2[inst] = acc[inst, ring_at(1 - inst, 2)].astype(bf16)
            send2(inst, 0).start()
            sc2[inst] = acc[inst, ring_at(1 - inst, -1)].astype(bf16)
            send2(inst, 2).start()

    def sum2_mid():
        for inst in range(2):
            send2(inst, 0).wait_recv()
            sb2[inst] = (acc[inst, ring_at(1 - inst, 1)] + ra2[inst].astype(f32)).astype(bf16)
            send2(inst, 1).start()

    def z_copy(j):
        to = yh * 4 + j
        slot = (to + 8 - z) % 8
        return to, rcopy(zs.at[j], zr.at[slot], zss.at[j], zrs.at[slot], at(x, y, to, core))

    def sum3_start():
        for inst in range(2):
            send2(inst, 1).wait_recv()
            send2(inst, 2).wait_recv()
            done = acc[inst, ring_at(1 - inst, 0)] + rb2[inst].astype(f32) + rc2[inst].astype(f32)
            for jj in range(2):
                j = inst * 2 + jj
                fin[j] = done[jj * 48 : jj * 48 + 48]
                zs[j] = done[jj * 48 : jj * 48 + 48].astype(bf16)
                to, copy = z_copy(j)
                pl.when(to != z)(copy.start)

    norm = 1.0 / math.sqrt(8 * 32 * TOK)
    keeper = z // 4 == yh

    def f_copy():
        return rcopy(fs, fr, fss.at[0], frs.at[0], final_mate)

    def sum_end():
        @pl.when(keeper)
        def _():
            total = fin[z % 4]
            for d in range(1, 8):
                rcopy(zs.at[0], zr.at[d], zss.at[0], zrs.at[d], sib).wait_recv()
                total = total + zr[d].astype(f32)
            total = total * norm
            left, right = total[:, 0:192], total[:, 192:384]
            dw_ref[...] = jnp.where(yh == 0, left, right)
            fs[...] = jnp.where(yh == 0, right, left)
            f_copy().start()

    def sum_last():
        @pl.when(jnp.logical_not(keeper))
        def _():
            f_copy().wait_recv()
            dw_ref[...] = fr[...]

    def backward(half, p, i):
        c = cols(p, 128)
        do = cot_win[half, :, cols(i, 128)]
        keys, values = kv_win[half, 0, :, c], kv_win[half, 1, :, c]
        q = q_win[half, :, c]
        prod = do.T.astype(f32) * o_f32[half, pl.ds(pl.multiple_of(p * 128, 128), 128), :]
        for h in range(2):
            grad = dot_nt(values, pick(do, h))
            total = jnp.sum(prod[64 * h : 64 * h + 64], axis=0, keepdims=True)
            ds_s[half, h] = (probs[half, p, h].astype(f32) * (grad - total)).astype(bf16)
        kt = keys.T
        dq = jnp.concatenate([dot(kt[64 * h : 64 * h + 64], ds_s[half, h]) for h in range(2)], axis=0) * 0.125
        dq_win[half, :, c] = dq.astype(bf16).T[0:BLK]
        dkv_win[half, 1, :, c] = (dot(probs[half, p, 0], pick(do, 0)) + dot(probs[half, p, 1], pick(do, 1))).astype(bf16)
        dkv_win[half, 0, :, c] = (dot(ds_s[half, 0], pick(q, 0)) + dot(ds_s[half, 1], pick(q, 1))).astype(bf16)

    order = (0, 1, 3, 2)

    def w_poll(*which):
        def poll():
            for piece in which:
                w_arrived(*piece)
            if (2, 0) in which:
                w_copy(2, 1).start()

        return poll

    polls = {
        (0, 0): [sum1_more, w_poll((1, 0), (1, 1))],
        (0, 2): [sum1_mid, w_poll((3, 0), (3, 1))],
        (1, 0): [w_poll((2, 0))],
        (1, 2): [sum2_start],
        (2, 0): [w_poll((2, 1))],
        (2, 2): [sum2_mid],
        (3, 1): [sum3_start],
    }

    def g_copy(to_next, k, part):
        first, width = ((0, 256), (256, 128))[part]
        c = pl.ds(pl.multiple_of(((x + 4 - order[k]) % 4) * GROUP + first, 128), width)
        i = 2 * k + part
        if to_next:
            return rcopy(dkv_win.at[1, :, BLK : 2 * BLK, c], rdkv.at[0, :, :, c], gs.at[0, i], gr.at[0, i], nxt)
        return rcopy(dkv_win.at[0, :, 0:BLK, c], rdkv.at[1, :, :, c], gs.at[1, i], gr.at[1, i], prev)

    def cotangent(k):
        d = order[k]
        for which in range(2):
            if d or which:
                w_sib(d, which).wait_recv()
        group = (x + 4 - d) % 4
        both = jnp.concatenate([dwin[0, 0:BLK, :], dwin[0, QP : QP + BLK, :]], axis=0)
        cot = dot_nt(both, w_all[pl.ds(pl.multiple_of(group * GROUP, GROUP), GROUP), :]).astype(bf16)
        cot_win[0, 0:BLK, :] = cot[0:BLK]
        cot_win[1, 0:BLK, :] = cot[BLK:]

    cotangent(0)
    weight_grad(1)
    sum1_start()
    for k, d in enumerate(order):
        if k:
            cotangent(k)
        for part in range(3):
            for half in range(2):
                backward(half, ((x + 4 - d) % 4) * 3 + part, part)
            if part:
                g_copy(True, k, part - 1).start()
                g_copy(False, k, part - 1).start()
            if (k, part) in polls:
                for poll in polls[k, part]:
                    poll()

    @pl.loop(0, 3)
    def _(i):
        c = cols(i, 512)
        w = w_all[:, c]
        first = dot(att_win[0], w)
        second = dot(att_win[1], w)
        dout_s[0:192, c] = first[0:192].astype(bf16)
        dout_s[192:208, c] = (first[192:208] + second[0:16]).astype(bf16)
        dout_s[208:392, c] = second[16:200].astype(bf16)

    out_mixed = pltpu.make_async_copy(dout_s, mixed_hbm, loc.at[5])
    out_mixed.start()
    qkv_s[0, 0:192, :] = dq_win[0, 0:192, :]
    qkv_s[0, 192:208, :] = dq_win[0, 192:208, :] + dq_win[1, 0:16, :]
    qkv_s[0, 208:392, :] = dq_win[1, 16:200, :]
    out_q = pltpu.make_async_copy(qkv_s.at[0], dqkv_hbm.at[0], loc.at[6])
    out_q.start()
    sum_end()
    for k in range(4):
        for part in range(2):
            g_copy(True, k, part).wait_recv()
            g_copy(False, k, part).wait_recv()
    outs = []
    for t in range(2):
        first = dkv_win[0, t, BLK:, :].astype(f32) + rdkv[0, t].astype(f32)
        second = dkv_win[1, t, 0:BLK, :].astype(f32) + rdkv[1, t].astype(f32)
        qkv_s[1 + t, 0:192, :] = first[0:192].astype(bf16)
        qkv_s[1 + t, 192:208, :] = (first[192:208] + second[0:16]).astype(bf16)
        qkv_s[1 + t, 208:392, :] = second[16:200].astype(bf16)
        outs.append(pltpu.make_async_copy(qkv_s.at[1 + t], dqkv_hbm.at[1 + t], loc.at[7 + t]))
        outs[t].start()
    sum_last()

    for piece in pieces:
        w_copy(*piece).wait_send()
        w_sib(*piece).wait_send()
    for c in range(STEPS):
        halo(True, c).wait_send()
        halo(False, c).wait_send()
    d_copy().wait_send()
    for half in range(2):
        o_copy(half).wait_send()
    for k in range(4):
        for part in range(2):
            g_copy(True, k, part).wait_send()
            g_copy(False, k, part).wait_send()
    for inst in range(2):
        for kind in range(3):
            send1(inst, kind).wait_send()
            send2(inst, kind).wait_send()
    for j in range(4):
        to, copy = z_copy(j)
        pl.when(to != z)(copy.wait_send)
    pl.when(keeper)(lambda: f_copy().wait_send())
    out_mixed.wait()
    out_q.wait()
    for out in outs:
        out.wait()


def settle(mixed_in, grads_in, weight_in, mixed_out, grads_out, weight_out, hold, hold_w, sems):
    ins = [pltpu.make_async_copy(mixed_in, hold.at[0], sems.at[0, 0])]
    outs = [pltpu.make_async_copy(hold.at[0], mixed_out, sems.at[1, 0])]
    for t in range(3):
        ins.append(pltpu.make_async_copy(grads_in.at[t], hold.at[1 + t], sems.at[0, 1 + t]))
        outs.append(pltpu.make_async_copy(hold.at[1 + t], grads_out.at[t], sems.at[1, 1 + t]))
    ins.append(pltpu.make_async_copy(weight_in, hold_w, sems.at[0, 4]))
    outs.append(pltpu.make_async_copy(hold_w, weight_out, sems.at[1, 4]))
    for copy in ins:
        copy.start()
    for copy, out in zip(ins, outs):
        copy.wait()
        out.start()
    for out in outs:
        out.wait()


def per_device(qkv, w_out, d_out, clip_ids):
    hbm = pl.BlockSpec(memory_space=pl.ANY)
    vmem = pltpu.VMEM
    dma = pltpu.SemaphoreType.DMA
    mixed, grads, d_weight = pl.pallas_call(
        kernel,
        in_specs=[hbm, hbm, hbm, pl.BlockSpec(memory_space=pltpu.SMEM)],
        out_specs=[hbm, hbm, pl.BlockSpec(memory_space=pltpu.VMEM)],
        out_shape=[
            jax.ShapeDtypeStruct((TOK, D), bf16),
            jax.ShapeDtypeStruct((3, TOK, D), bf16),
            jax.ShapeDtypeStruct((48, 192), f32),
        ],
        scratch_shapes=[
            vmem((3, TOK, D), bf16),
            vmem((TOK, D), bf16),
            vmem((2, 2, 2 * BLK, D), bf16),
            vmem((2, QP, D), bf16),
            vmem((2, 2 * QP, D), bf16),
            vmem((D, D), bf16),
            vmem((2, PAIRS, 2, 2 * BLK, QP), bf16),
            vmem((2, D, QP), f32),
            vmem((16, 6, 16, 4 * QP), bf16),
            vmem((2, BLK, D), bf16),
            vmem((2, QP, GROUP), bf16),
            vmem((2, 2, 2 * BLK, QP), bf16),
            vmem((2, 2, 2 * BLK, D), bf16),
            vmem((2, 2, BLK, D), bf16),
            vmem((2, BLK, D), bf16),
            vmem((2, 2 * BLK, 128), bf16),
            vmem((2, QP, 128), bf16),
            vmem((4, 768, GROUP), f32),
            vmem((2, 4, 96, GROUP), f32),
        ]
        + [vmem((2, 4, 96, GROUP), bf16)] * 6
        + [vmem((2, 96, GROUP), bf16)] * 6
        + [
            vmem((4, 48, GROUP), f32),
            vmem((4, 48, GROUP), bf16),
            vmem((8, 48, GROUP), bf16),
            vmem((48, 192), f32),
            vmem((48, 192), f32),
            dma((9,)),
            dma((2, STEPS)), dma((2, STEPS)),
            dma((4, 2)), dma((4, 2)), dma((4, 2)), dma((4, 2)),
            dma((1,)), dma((1,)), dma((2,)), dma((2,)),
            dma((2, 8)), dma((2, 8)),
            dma((2, 3)), dma((2, 3)), dma((2, 3)), dma((2, 3)),
            dma((4,)), dma((8,)), dma((1,)), dma((1,)),
        ],
        compiler_params=pltpu.CompilerParams(
            collective_id=0, has_side_effects=True, vmem_limit_bytes=62 << 20
        ),
    )(qkv[0], w_out, d_out[0], clip_ids)
    mixed, grads, d_weight = pl.pallas_call(
        settle,
        in_specs=[hbm] * 3,
        out_specs=[hbm] * 3,
        out_shape=[
            jax.ShapeDtypeStruct((TOK, D), bf16),
            jax.ShapeDtypeStruct((3, TOK, D), bf16),
            jax.ShapeDtypeStruct((48, 192), f32),
        ],
        scratch_shapes=[vmem((4, TOK, D), bf16), vmem((48, 192), f32), dma((2, 5))],
        compiler_params=pltpu.CompilerParams(vmem_limit_bytes=62 << 20),
    )(mixed, grads, d_weight)
    return mixed[None], grads[None], d_weight


def solution(mesh):
    return jax.shard_map(
        per_device,
        mesh=mesh,
        in_specs=(P("dp", None, "tm", None), P("dp", None), P("dp", "tm", None), P("dp", None)),
        out_specs=(P("dp", "tm", None), P("dp", None, "tm", None), P("tm", "dp")),
        check_vma=False,
    )
```

```python
import functools
import math

import jax
import jax.numpy as jnp
from jax import lax
from jax.experimental import pallas as pl
from jax.experimental.pallas import tpu as pltpu
from jax.sharding import PartitionSpec as P

MESH = pl.DeviceIdType.MESH
f32, bf16 = jnp.float32, jnp.bfloat16

HEADS = 24
HEAD_DIM = 64
D = 1536
SPATIAL = 49
WIN_T = 8
FRAMES = 256
TOK = 392
HALF = 196
BLK = 208
LO = 192
QP = 256
PAIRS = HEADS // 2
CHUNK = 256
STEPS = D // CHUNK
PER = CHUNK // 128
GROUP = 384
NEG = -1e30
NT = (((1,), (1,)), ((), ()))


def dot(a, b):
    return jnp.dot(a, b, preferred_element_type=f32)


def dot_nt(a, b):
    return lax.dot_general(a, b, NT, preferred_element_type=f32)


def frame_of(row):
    frame = jnp.zeros_like(row)
    for i in range(1, WIN_T):
        frame = frame + jnp.where(row >= SPATIAL * i, 1, 0)
    return frame


def cols(p, width):
    return pl.ds(pl.multiple_of(p * width, 128), width)


def kernel(
    qkv_hbm, w_hbm, dout_hbm, clip_ref,
    mixed_hbm, dqkv_hbm, dw_ref,
    qkv_s, dout_s, kv_win, q_win, dwin, w_all, probs, o_f32, o_rows, att_win,
    cot_win, ds_s, dkv_win, rdkv, dq_win, kaug, qaug,
    g_all, acc, sa1, sb1, sc1, ra1, rb1, rc1, sa2, sb2, sc2, ra2, rb2, rc2,
    fin, zs, zr, fs, fr,
    loc, hs, hr, ws, wr, wbs, wbr, ds_sem, dr_sem, os_sem, or_sem,
    gs, gr, r1s, r1r, r2s, r2r, zss, zrs, fss, frs,
):
    dp, tm = lax.axis_index("dp"), lax.axis_index("tm")
    x, yh = dp // 2, dp % 2
    yl, z, core = tm // 16, (tm // 2) % 8, tm % 2
    y = yh * 2 + yl
    step = 1 - 2 * core

    def at(x_, y_, z_, c_):
        return (x_ * 2 + y_ // 2, (y_ % 2) * 16 + z_ * 2 + c_)

    def along_x(d):
        return at((x + d + 4) % 4, y, z, core)

    def along_y(d):
        return at(x, (y + d + 4) % 4, z, core)

    prev, nxt = (dp, (tm + 31) % 32), (dp, (tm + 1) % 32)
    sib = (dp, tm + step)
    final_mate = (dp + 1 - 2 * yh, tm)

    across = at(x, 3 - y, z, core)

    def rcopy(src, dst, ssem, rsem, dev):
        return pltpu.make_async_remote_copy(
            src_ref=src, dst_ref=dst, send_sem=ssem, recv_sem=rsem, device_id=dev, device_id_type=MESH
        )

    loads = [
        pltpu.make_async_copy(qkv_hbm.at[1], qkv_s.at[1], loc.at[1]),
        pltpu.make_async_copy(qkv_hbm.at[2], qkv_s.at[2], loc.at[2]),
        pltpu.make_async_copy(qkv_hbm.at[0], qkv_s.at[0], loc.at[0]),
        pltpu.make_async_copy(dout_hbm, dout_s, loc.at[3]),
        pltpu.make_async_copy(
            w_hbm, w_all.at[pl.ds(pl.multiple_of(dp * 192, 192), 192)], loc.at[4]
        ),
    ]
    for load in loads:
        load.start()

    barrier = pltpu.get_barrier_semaphore()
    peers = [prev, nxt, along_x(1), along_x(2), along_x(3), along_y(1), along_y(2), along_y(3)]
    peers += [at(x, y, (z + d) % 8, core) for d in range(1, 8)]
    for dev in peers:
        pl.semaphore_signal(barrier, inc=1, device_id=dev, device_id_type=MESH)

    def w_rows(d, which):
        src = ((x + 4 - d) % 4) * 2 + (yh if which == 0 else 1 - yh)
        return w_all.at[pl.ds(pl.multiple_of(src * 192 + core * 96, 96), 96)]

    def w_copy(d, which):
        if (d, which) == (0, 1):
            rows, dev = w_rows(0, 0), across
        elif (d, which) == (2, 1):
            rows, dev = w_rows(2, 0), across
        else:
            rows, dev = w_rows(0, which), along_x(d)
        return rcopy(rows, rows, ws.at[d, which], wr.at[d, which], dev)

    def w_sib(d, which):
        rows = w_rows(d, which)
        return rcopy(rows, rows, wbs.at[d, which], wbr.at[d, which], sib)

    def w_arrived(d, which):
        w_copy(d, which).wait_recv()
        w_sib(d, which).start()

    pieces = [(0, 1)] + [(d, which) for d in (1, 3, 2) for which in range(2)]

    loads[0].wait()
    loads[1].wait()
    for t in range(2):
        kv_win[0, t, BLK:, :] = qkv_s[1 + t, 0:BLK, :]
        kv_win[1, t, 0:192, :] = qkv_s[1 + t, LO:384, :]
        kv_win[1, t, 192:200, :] = qkv_s[1 + t, 384:392, :]
        kv_win[1, t, 200:208, :] = jnp.zeros((8, D), bf16)

    def halo(to_next, c):
        if to_next:
            part = kv_win.at[1, :, 0:BLK, c * CHUNK : (c + 1) * CHUNK]
            there = kv_win.at[0, :, 0:BLK, c * CHUNK : (c + 1) * CHUNK]
            return rcopy(part, there, hs.at[0, c], hr.at[0, c], nxt)
        part = kv_win.at[0, :, BLK : 2 * BLK, c * CHUNK : (c + 1) * CHUNK]
        there = kv_win.at[1, :, BLK : 2 * BLK, c * CHUNK : (c + 1) * CHUNK]
        return rcopy(part, there, hs.at[1, c], hr.at[1, c], prev)

    pl.semaphore_wait(barrier, len(peers))
    for c in range(STEPS):
        halo(True, c).start()
        halo(False, c).start()
    loads[4].wait()
    for piece in ((0, 1), (1, 0), (3, 0), (2, 0)):
        w_copy(*piece).start()

    loads[2].wait()
    q_win[0, 0:BLK, :] = qkv_s[0, 0:BLK, :] * jnp.asarray(0.125, bf16)
    q_win[1, 0:192, :] = qkv_s[0, LO:384, :] * jnp.asarray(0.125, bf16)
    q_win[1, 192:200, :] = qkv_s[0, 384:392, :] * jnp.asarray(0.125, bf16)
    q_win[1, 200:208, :] = jnp.zeros((8, D), bf16)
    q_win[:, BLK:, :] = jnp.zeros((2, QP - BLK, D), bf16)

    loads[3].wait()
    row16 = lax.broadcasted_iota(jnp.int32, (16, D), 0)
    zero16 = jnp.zeros((16, D), f32)
    edge = dout_s[192:208, :].astype(f32)
    dwin[0, 0:192, :] = dout_s[0:192, :]
    dwin[0, 192:208, :] = jnp.where(row16 < HALF - LO, edge, zero16).astype(bf16)
    dwin[0, 208:256, :] = jnp.zeros((48, D), bf16)
    dwin[0, 256:272, :] = jnp.where(row16 >= HALF - LO, edge, zero16).astype(bf16)
    dwin[0, 272:448, :] = dout_s[208:384, :]
    dwin[0, 448:456, :] = dout_s[384:392, :]
    dwin[0, 456:464, :] = jnp.zeros((8, D), bf16)
    dwin[0, 464:512, :] = jnp.zeros((48, D), bf16)
    cot_win[:, BLK:, :] = jnp.zeros((2, QP - BLK, GROUP), bf16)

    def d_copy():
        return rcopy(dwin.at[0], dwin.at[1], ds_sem.at[0], dr_sem.at[0], sib)

    d_copy().start()

    row = lax.broadcasted_iota(jnp.int32, (BLK, 128), 0)
    lane = lax.broadcasted_iota(jnp.int32, (BLK, 128), 1)
    row_q = lax.broadcasted_iota(jnp.int32, (QP, 128), 0)
    lane_q = lax.broadcasted_iota(jnp.int32, (QP, 128), 1)
    for half in range(2):
        clips = [clip_ref[0, (tm * 8 + FRAMES - 4 + 8 * half + w) % FRAMES] for w in range(WIN_T)]
        of_lane = jnp.full((BLK, 128), -1, jnp.int32)
        for w in range(WIN_T):
            of_lane = jnp.where(lane == w, clips[w], of_lane)
        for part in range(2):
            if part == 0:
                frame, real = frame_of(row + LO) - 4, jnp.logical_and(row >= HALF - LO, row < TOK - LO)
            else:
                frame, real = frame_of(row) + 4, row < HALF
            of_row = jnp.full((BLK, 128), -2, jnp.int32)
            for w in range(WIN_T):
                of_row = jnp.where(frame == w, clips[w], of_row)
            seen = jnp.logical_and(real, of_row == of_lane)
            bias = jnp.where(jnp.logical_or(seen, lane >= WIN_T), 0.0, NEG)
            kaug[half, part * BLK : (part + 1) * BLK, :] = bias.astype(bf16)
        if half == 0:
            frame, real = frame_of(row_q) + 4, row_q < HALF
        else:
            frame = frame_of(row_q + LO) - 4
            real = jnp.logical_and(row_q >= HALF - LO, row_q < TOK - LO)
        qaug[half] = jnp.where(jnp.logical_and(real, lane_q == frame), 1.0, 0.0).astype(bf16)

    low = lane_q < HEAD_DIM
    none = jnp.zeros((QP, 128), bf16)
    q_lane = lax.broadcasted_iota(jnp.int32, (1, QP), 1)

    def pick(value, h):
        return jnp.where(low, value, none) if h == 0 else jnp.where(low, none, value)

    def softmax(half, p):
        c = cols(p, 128)
        q = q_win[half, :, c]
        keys = jnp.concatenate([kv_win[half, 0, :, c], kaug[half]], axis=1)
        marks = qaug[half]
        for h in range(2):
            s = dot_nt(keys, jnp.concatenate([pick(q, h), marks], axis=1))
            e = jnp.exp(s - jnp.max(s, axis=0, keepdims=True))
            total = jnp.sum(e, axis=0, keepdims=True)
            probs[half, p, h] = (e * (1.0 / total)).astype(bf16)

    def attend(half, p):
        c = cols(p, 128)
        start = jnp.where(half == 0, 0, HALF - LO)
        valid = jnp.logical_and(q_lane >= start, q_lane < start + HALF).astype(f32)
        vt = kv_win[half, 1, :, c].T
        outs = []
        for h in range(2):
            outs.append(dot(vt[64 * h : 64 * h + 64], probs[half, p, h]) * valid)
        o = jnp.concatenate(outs, axis=0)
        o_f32[half, pl.ds(pl.multiple_of(p * 128, 128), 128), :] = o
        low_o = o.astype(bf16)
        for j in range(8):
            r = p * 8 + j
            o_rows[r // 6, r % 6, :, cols(half, QP)] = low_o[16 * j : 16 * j + 16]
        att_win[half, :, c] = low_o.T[0:BLK]

    def o_copy(half):
        rows = pl.ds(3 * (1 - core), 3)
        return rcopy(
            o_rows.at[:, rows, :, cols(half, QP)],
            o_rows.at[:, rows, :, pl.ds(pl.multiple_of(512 + half * QP, QP), QP)],
            os_sem.at[half], or_sem.at[half], sib,
        )

    def weight_grad(turn):
        own, there = (1 - core, core) if turn == 0 else (core, 1 - core)
        o_copy(there).wait_recv()

        @pl.loop(0, 4)
        def _(i):
            sub = pl.ds(3 * core, 3)
            lhs = jnp.concatenate(
                [
                    o_rows[:, sub, :, cols(own, QP)].reshape(768, QP),
                    o_rows[:, sub, :, pl.ds(pl.multiple_of(512 + there * QP, QP), QP)].reshape(768, QP),
                ],
                axis=1,
            )
            rhs = jnp.concatenate(
                [
                    dwin[0, pl.ds(pl.multiple_of(own * QP, QP), QP), cols(i, GROUP)],
                    dwin[1, pl.ds(pl.multiple_of(there * QP, QP), QP), cols(i, GROUP)],
                ],
                axis=0,
            )
            if turn == 0:
                g_all[i] = dot(lhs, rhs)
            else:
                g_all[i] += dot(lhs, rhs)

    for turn in range(2):
        half = 1 - core if turn == 0 else core
        for c in range(STEPS):
            pltpu.make_async_remote_copy(
                src_ref=kv_win.at[0, :, 0:BLK, 0:CHUNK],
                dst_ref=kv_win.at[half, :, pl.ds(pl.multiple_of(half * BLK, BLK), BLK), c * CHUNK : (c + 1) * CHUNK],
                send_sem=hs.at[0, c], recv_sem=hr.at[half, c], device_id=nxt, device_id_type=MESH,
            ).wait_recv()

            for p in range(c * PER, (c + 1) * PER):
                if c:
                    attend(half, p - PER)
            for p in range(c * PER, (c + 1) * PER):
                softmax(half, p)
            if c == STEPS - 1:
                for p in range(c * PER, (c + 1) * PER):
                    attend(half, p)

            if turn == 0 and c == 5:
                w_arrived(0, 1)
                w_copy(1, 1).start()
                w_copy(3, 1).start()
            if turn == 1 and c == 1:
                d_copy().wait_recv()
                weight_grad(0)
        o_copy(half).start()

    def ring_dev(axis, d):
        return along_y(d) if axis == 0 else along_x(d)

    def ring_at(axis, d):
        if axis == 0:
            to = (y + 4 + d * step) % 4
            return (to % 2) * 2 + to // 2
        return (x + 4 + d * step) % 4

    def piece1(inst, d):
        where = ring_at(inst, d)
        if inst == 0:
            return g_all[:, pl.ds(pl.multiple_of(where * 192, 96), 96), :]
        return jnp.stack([g_all[where, r * 192 + 96 : r * 192 + 192, :] for r in range(4)])

    def send1(inst, kind):
        src, dst = ((sa1, ra1), (sb1, rb1), (sc1, rc1))[kind]
        dev = ring_dev(inst, step if kind < 2 else -step)
        return rcopy(src.at[inst], dst.at[inst], r1s.at[inst, kind], r1r.at[inst, kind], dev)

    def send2(inst, kind):
        src, dst = ((sa2, ra2), (sb2, rb2), (sc2, rc2))[kind]
        dev = ring_dev(1 - inst, step if kind < 2 else -step)
        return rcopy(src.at[inst], dst.at[inst], r2s.at[inst, kind], r2r.at[inst, kind], dev)

    def sum1_start():
        for inst in range(2):
            sa1[inst] = piece1(inst, 2).astype(bf16)
            send1(inst, 0).start()

        for inst in range(2):
            sc1[inst] = piece1(inst, -1).astype(bf16)
            send1(inst, 2).start()

    def sum1_mid():
        for inst in range(2):
            send1(inst, 0).wait_recv()
            sb1[inst] = (piece1(inst, 1) + ra1[inst].astype(f32)).astype(bf16)
            send1(inst, 1).start()

    def sum2_start():
        for inst in range(2):
            send1(inst, 1).wait_recv()
            send1(inst, 2).wait_recv()
            acc[inst] = piece1(inst, 0) + rb1[inst].astype(f32) + rc1[inst].astype(f32)
            sa2[inst] = acc[inst, ring_at(1 - inst, 2)].astype(bf16)
            send2(inst, 0).start()
            sc2[inst] = acc[inst, ring_at(1 - inst, -1)].astype(bf16)
            send2(inst, 2).start()

    def sum2_mid():
        for inst in range(2):
            send2(inst, 0).wait_recv()
            sb2[inst] = (acc[inst, ring_at(1 - inst, 1)] + ra2[inst].astype(f32)).astype(bf16)
            send2(inst, 1).start()

    def z_copy(j):
        to = yh * 4 + j
        slot = (to + 8 - z) % 8
        return to, rcopy(zs.at[j], zr.at[slot], zss.at[j], zrs.at[slot], at(x, y, to, core))

    def sum3_start():
        for inst in range(2):
            send2(inst, 1).wait_recv()
            send2(inst, 2).wait_recv()
            done = acc[inst, ring_at(1 - inst, 0)] + rb2[inst].astype(f32) + rc2[inst].astype(f32)
            for jj in range(2):
                j = inst * 2 + jj
                fin[j] = done[jj * 48 : jj * 48 + 48]
                zs[j] = done[jj * 48 : jj * 48 + 48].astype(bf16)
                to, copy = z_copy(j)
                pl.when(to != z)(copy.start)

    norm = 1.0 / math.sqrt(8 * 32 * TOK)
    keeper = z // 4 == yh

    def f_copy():
        return rcopy(fs, fr, fss.at[0], frs.at[0], final_mate)

    def sum_end():
        @pl.when(keeper)
        def _():
            total = fin[z % 4]
            for d in range(1, 8):
                rcopy(zs.at[0], zr.at[d], zss.at[0], zrs.at[d], sib).wait_recv()
                total = total + zr[d].astype(f32)
            total = total * norm
            left, right = total[:, 0:192], total[:, 192:384]
            dw_ref[...] = jnp.where(yh == 0, left, right)
            fs[...] = jnp.where(yh == 0, right, left)
            f_copy().start()

    def sum_last():
        @pl.when(jnp.logical_not(keeper))
        def _():
            f_copy().wait_recv()
            dw_ref[...] = fr[...]

    def score_grad(half, p, i):
        c = cols(p, 128)
        do = cot_win[half, :, cols(i, 128)]
        values = kv_win[half, 1, :, c]
        prod = do.T.astype(f32) * o_f32[half, pl.ds(pl.multiple_of(p * 128, 128), 128), :]
        for h in range(2):
            grad = dot_nt(values, pick(do, h))
            total = jnp.sum(prod[64 * h : 64 * h + 64], axis=0, keepdims=True)
            ds_s[half, h] = (probs[half, p, h].astype(f32) * (grad - total)).astype(bf16)

    def both_heads(first, second, rhs):
        lhs = jnp.concatenate([first, second], axis=1)
        return dot(lhs, jnp.concatenate([pick(rhs, 0), pick(rhs, 1)], axis=0)).astype(bf16)

    def products(half, p, i):
        c = cols(p, 128)
        do = cot_win[half, :, cols(i, 128)]
        dkv_win[half, 1, :, c] = both_heads(probs[half, p, 0], probs[half, p, 1], do)
        dkv_win[half, 0, :, c] = both_heads(ds_s[half, 0], ds_s[half, 1], q_win[half, :, c])
        kt = kv_win[half, 0, :, c].T
        dq = jnp.concatenate([dot(kt[64 * h : 64 * h + 64], ds_s[half, h]) for h in range(2)], axis=0) * 0.125
        dq_win[half, :, c] = dq.astype(bf16).T[0:BLK]

    order = (0, 1, 3, 2)

    def w_poll(*which):
        def poll():
            for piece in which:
                w_arrived(*piece)
            if (2, 0) in which:
                w_copy(2, 1).start()

        return poll

    polls = {
        (0, 0): [w_poll((1, 0), (1, 1))],
        (0, 2): [sum1_mid, w_poll((3, 0), (3, 1))],
        (1, 0): [w_poll((2, 0))],
        (1, 2): [sum2_start],
        (2, 0): [w_poll((2, 1))],
        (2, 1): [sum2_mid],
        (3, 0): [sum3_start],
    }

    def g_copy(to_next, k, part):
        first, width = ((0, 256), (256, 128))[part]
        c = pl.ds(pl.multiple_of(((x + 4 - order[k]) % 4) * GROUP + first, 128), width)
        i = 2 * k + part
        if to_next:
            return rcopy(dkv_win.at[1, :, BLK : 2 * BLK, c], rdkv.at[0, :, :, c], gs.at[0, i], gr.at[0, i], nxt)
        return rcopy(dkv_win.at[0, :, 0:BLK, c], rdkv.at[1, :, :, c], gs.at[1, i], gr.at[1, i], prev)

    def cotangent(k):
        d = order[k]
        for which in range(2):
            if d or which:
                w_sib(d, which).wait_recv()
        group = (x + 4 - d) % 4
        both = jnp.concatenate([dwin[0, 0:BLK, :], dwin[0, QP : QP + BLK, :]], axis=0)
        cot = dot_nt(both, w_all[pl.ds(pl.multiple_of(group * GROUP, GROUP), GROUP), :]).astype(bf16)
        cot_win[0, 0:BLK, :] = cot[0:BLK]
        cot_win[1, 0:BLK, :] = cot[BLK:]

    cotangent(0)
    weight_grad(1)
    sum1_start()
    for k, d in enumerate(order):
        if k:
            cotangent(k)
        for part in range(3):
            pair = ((x + 4 - d) % 4) * 3 + part
            score_grad(0, pair, part)
            score_grad(1, pair, part)
            products(0, pair, part)
            products(1, pair, part)
            if part:
                g_copy(True, k, part - 1).start()
                g_copy(False, k, part - 1).start()
            if (k, part) in polls:
                for poll in polls[k, part]:
                    poll()

    @pl.loop(0, 3)
    def _(i):
        c = cols(i, 512)
        w = w_all[:, c]
        both = dot(att_win[...].reshape(2 * BLK, D), w)
        first, second = both[0:BLK], both[BLK:]
        dout_s[0:192, c] = first[0:192].astype(bf16)
        dout_s[192:208, c] = (first[192:208] + second[0:16]).astype(bf16)
        dout_s[208:392, c] = second[16:200].astype(bf16)

    out_mixed = pltpu.make_async_copy(dout_s, mixed_hbm, loc.at[5])
    out_mixed.start()
    qkv_s[0, 0:192, :] = dq_win[0, 0:192, :]
    qkv_s[0, 192:208, :] = dq_win[0, 192:208, :] + dq_win[1, 0:16, :]
    qkv_s[0, 208:392, :] = dq_win[1, 16:200, :]
    out_q = pltpu.make_async_copy(qkv_s.at[0], dqkv_hbm.at[0], loc.at[6])
    out_q.start()
    sum_end()
    for k in range(4):
        for part in range(2):
            g_copy(True, k, part).wait_recv()
            g_copy(False, k, part).wait_recv()
    outs = []
    for t in range(2):
        first = dkv_win[0, t, BLK:, :].astype(f32) + rdkv[0, t].astype(f32)
        second = dkv_win[1, t, 0:BLK, :].astype(f32) + rdkv[1, t].astype(f32)
        qkv_s[1 + t, 0:192, :] = first[0:192].astype(bf16)
        qkv_s[1 + t, 192:208, :] = (first[192:208] + second[0:16]).astype(bf16)
        qkv_s[1 + t, 208:392, :] = second[16:200].astype(bf16)
        outs.append(pltpu.make_async_copy(qkv_s.at[1 + t], dqkv_hbm.at[1 + t], loc.at[7 + t]))
        outs[t].start()
    sum_last()

    for piece in pieces:
        w_copy(*piece).wait_send()
        w_sib(*piece).wait_send()
    for c in range(STEPS):
        halo(True, c).wait_send()
        halo(False, c).wait_send()
    d_copy().wait_send()
    for half in range(2):
        o_copy(half).wait_send()
    for k in range(4):
        for part in range(2):
            g_copy(True, k, part).wait_send()
            g_copy(False, k, part).wait_send()
    for inst in range(2):
        for kind in range(3):
            send1(inst, kind).wait_send()
            send2(inst, kind).wait_send()
    for j in range(4):
        to, copy = z_copy(j)
        pl.when(to != z)(copy.wait_send)
    pl.when(keeper)(lambda: f_copy().wait_send())
    out_mixed.wait()
    out_q.wait()
    for out in outs:
        out.wait()


def settle(mixed_in, grads_in, weight_in, mixed_out, grads_out, weight_out, hold, hold_w, sems):
    ins = [pltpu.make_async_copy(mixed_in, hold.at[0], sems.at[0, 0])]
    outs = [pltpu.make_async_copy(hold.at[0], mixed_out, sems.at[1, 0])]
    for t in range(3):
        ins.append(pltpu.make_async_copy(grads_in.at[t], hold.at[1 + t], sems.at[0, 1 + t]))
        outs.append(pltpu.make_async_copy(hold.at[1 + t], grads_out.at[t], sems.at[1, 1 + t]))
    ins.append(pltpu.make_async_copy(weight_in, hold_w, sems.at[0, 4]))
    outs.append(pltpu.make_async_copy(hold_w, weight_out, sems.at[1, 4]))
    for copy in ins:
        copy.start()
    for copy, out in zip(ins, outs):
        copy.wait()
        out.start()
    for out in outs:
        out.wait()


def per_device(qkv, w_out, d_out, clip_ids):
    hbm = pl.BlockSpec(memory_space=pl.ANY)
    vmem = pltpu.VMEM
    dma = pltpu.SemaphoreType.DMA
    mixed, grads, d_weight = pl.pallas_call(
        kernel,
        in_specs=[hbm, hbm, hbm, pl.BlockSpec(memory_space=pltpu.SMEM)],
        out_specs=[hbm, hbm, pl.BlockSpec(memory_space=pltpu.VMEM)],
        out_shape=[
            jax.ShapeDtypeStruct((TOK, D), bf16),
            jax.ShapeDtypeStruct((3, TOK, D), bf16),
            jax.ShapeDtypeStruct((48, 192), f32),
        ],
        scratch_shapes=[
            vmem((3, TOK, D), bf16),
            vmem((TOK, D), bf16),
            vmem((2, 2, 2 * BLK, D), bf16),
            vmem((2, QP, D), bf16),
            vmem((2, 2 * QP, D), bf16),
            vmem((D, D), bf16),
            vmem((2, PAIRS, 2, 2 * BLK, QP), bf16),
            vmem((2, D, QP), f32),
            vmem((16, 6, 16, 4 * QP), bf16),
            vmem((2, BLK, D), bf16),
            vmem((2, QP, GROUP), bf16),
            vmem((2, 2, 2 * BLK, QP), bf16),
            vmem((2, 2, 2 * BLK, D), bf16),
            vmem((2, 2, BLK, D), bf16),
            vmem((2, BLK, D), bf16),
            vmem((2, 2 * BLK, 128), bf16),
            vmem((2, QP, 128), bf16),
            vmem((4, 768, GROUP), f32),
            vmem((2, 4, 96, GROUP), f32),
        ]
        + [vmem((2, 4, 96, GROUP), bf16)] * 6
        + [vmem((2, 96, GROUP), bf16)] * 6
        + [
            vmem((4, 48, GROUP), f32),
            vmem((4, 48, GROUP), bf16),
            vmem((8, 48, GROUP), bf16),
            vmem((48, 192), f32),
            vmem((48, 192), f32),
            dma((9,)),
            dma((2, STEPS)), dma((2, STEPS)),
            dma((4, 2)), dma((4, 2)), dma((4, 2)), dma((4, 2)),
            dma((1,)), dma((1,)), dma((2,)), dma((2,)),
            dma((2, 8)), dma((2, 8)),
            dma((2, 3)), dma((2, 3)), dma((2, 3)), dma((2, 3)),
            dma((4,)), dma((8,)), dma((1,)), dma((1,)),
        ],
        compiler_params=pltpu.CompilerParams(
            collective_id=0, has_side_effects=True, vmem_limit_bytes=62 << 20
        ),
    )(qkv[0], w_out, d_out[0], clip_ids)
    mixed, grads, d_weight = pl.pallas_call(
        settle,
        in_specs=[hbm] * 3,
        out_specs=[hbm] * 3,
        out_shape=[
            jax.ShapeDtypeStruct((TOK, D), bf16),
            jax.ShapeDtypeStruct((3, TOK, D), bf16),
            jax.ShapeDtypeStruct((48, 192), f32),
        ],
        scratch_shapes=[vmem((4, TOK, D), bf16), vmem((48, 192), f32), dma((2, 5))],
        compiler_params=pltpu.CompilerParams(vmem_limit_bytes=62 << 20),
    )(mixed, grads, d_weight)
    return mixed[None], grads[None], d_weight


def solution(mesh):
    return jax.shard_map(
        per_device,
        mesh=mesh,
        in_specs=(P("dp", None, "tm", None), P("dp", None), P("dp", "tm", None), P("dp", None)),
        out_specs=(P("dp", "tm", None), P("dp", None, "tm", None), P("tm", "dp")),
        check_vma=False,
    )
```
